128 devices in a mesh: node: 64 (over z, y, x), feat: 2 (over core).
Axes of the slice: x: 4, y: 4, z: 4, core: 2. Of those that a mesh axis runs over, the one named last changes fastest.
Arguments:
- features: bfloat16 [327680, 1024], P('node', 'feat'), may hold values from -6 to 6
- upstream: bfloat16 [327680, 1024], P('node', 'feat'), may hold values from -6 to 6
- preact: bfloat16 [327680, 1024], P('node', 'feat'), may hold values from -6 to 6
- adj_tiles: bfloat16 [5120, 128, 128], P('node'), may hold values from 0 to 0.14941406
- tile_source: int32 [5120], P('node'), may hold values from 0 to 119
Outputs:
- weight_grad: float32 [1024, 1024], P('feat', 'node')
The draws below stay inside these ranges and needn't reach their ends.
All inputs are finite; a program needn't handle non-finite values.
Results may differ from the reference program's by a relative error of at most 0.0022.
Values may be sent and summed in bfloat16 or wider, within the bound.
A program may use at most 256 MiB of HBM per device.

```python
import jax
import jax.numpy as jnp
from jax import lax

F = 1024
HID = 1024
TB = 128
TILE_PER = 2
BLK = 40
NODES = 327680
TILES = 5120
N_NODE = 64


def with_ends(array, key, smallest, high):
    longest = array.shape.index(max(array.shape))
    spots = []
    for shift in (0, 1):
        where = [jax.random.randint(jax.random.fold_in(key, axis), (), 0, length) for axis, length in enumerate(array.shape)]
        where[longest] = (where[longest] + shift) % array.shape[longest]
        spots.append(tuple(where))
    return array.at[spots[0]].set(smallest).at[spots[1]].set(high)


def block_levels(stream_key, shape, shards, low, top_value):
    loudness = 1.0
    for axis_at, shards_of in shards:
        draws = jax.random.uniform(jax.random.fold_in(jax.random.fold_in(stream_key, 6), axis_at), (shards_of,), jnp.float32, low / len(shards), top_value / len(shards))
        loudness = loudness * jnp.repeat(jnp.exp(draws), shape[axis_at] // shards_of).reshape((-1,) + (1,) * (len(shape) - 1 - axis_at))
    return loudness


def gaussian(own_key, extent, width, bound, pieces=(), kind=jnp.bfloat16):
    result = jax.random.normal(own_key, extent, jnp.float32) * width
    if len(pieces) > 0:
        result = block_levels(own_key, extent, pieces, -0.22, 0.18) * result
    return jnp.clip(result, min=-bound, max=bound).astype(kind)


def setup_inputs(seed: int = 0) -> dict:
    streams_of = jax.random.split(jax.random.key(seed), 6)
    features = gaussian(streams_of[0], (NODES, F), 1.0, 6.0, ((0, 64), (1, 2)))
    upstream = gaussian(streams_of[1], (NODES, HID), 1.0, 6.0, ((0, 64), (1, 2)))
    preact = gaussian(streams_of[2], (NODES, HID), 1.0, 6.0, ((0, 64), (1, 2)))
    adj_tiles = jnp.clip(0.14941406 * jax.random.uniform(streams_of[3], (TILES, TB, TB), jnp.float32) ** block_levels(streams_of[3], (TILES, TB, TB), ((0, 64),), -0.2, 0.2), 0.0, 0.14941406).astype(jnp.bfloat16)
    tile_source = with_ends(jax.random.randint(streams_of[4], (TILES,), 0, 3 * BLK), jax.random.fold_in(streams_of[4], 1), 0, (3 * BLK) - 1).astype(jnp.int32)
    return {"features": features, "upstream": upstream, "preact": preact, "adj_tiles": adj_tiles, "tile_source": tile_source}


def reference(features, upstream, preact, adj_tiles, tile_source):
    grad_out = jnp.where(preact > 0, upstream, jnp.zeros_like(upstream))
    out_blocks = grad_out.reshape(N_NODE, BLK, TB, HID)
    tile_view = adj_tiles.reshape(N_NODE, BLK, TILE_PER, TB, TB)
    sources = tile_source.reshape(N_NODE, BLK * TILE_PER)

    def shard_step(totals, shard_index):
        contrib = jnp.einsum("bpds,bdh->bpsh", tile_view[shard_index].astype(jnp.float32), out_blocks[shard_index].astype(jnp.float32))
        contrib = contrib.reshape(BLK * TILE_PER, TB, HID)
        local_src = sources[shard_index]
        owner_shard = (shard_index + local_src // BLK - 1 + N_NODE) % N_NODE
        global_block = (owner_shard * BLK + local_src % BLK).astype(jnp.int32)
        return totals.at[global_block].add(contrib), None

    start_sums = jnp.zeros((N_NODE * BLK, TB, HID), jnp.float32)
    totals, unused = lax.scan(shard_step, start_sums, jnp.arange(N_NODE, dtype=jnp.int32))
    grad_z = totals.reshape(NODES, HID)
    factor = float(NODES) ** -0.5
    dims = (((0,), (0,)), ((), ()))
    product = lax.dot_general(features.astype(jnp.float32), grad_z, dims, precision=lax.Precision.HIGHEST, preferred_element_type=jnp.float32)
    return product * factor
```

```python
import functools

import jax
import jax.numpy as jnp
from jax import lax
from jax.experimental import pallas as pl
from jax.experimental.pallas import tpu as pltpu
from jax.sharding import PartitionSpec as P

MESH = pl.DeviceIdType.MESH
SIDE = 4
TILE = 128
COLS = 128
ROWS = 512


def fused_kernel(cap, *refs):
    refs = list(refs)
    features, upstream, preact, adj_hbm, where, to_upper, to_lower, out = refs[:8]
    refs = refs[8:]
    stages = features.shape[2] // COLS
    own, refs = refs[:stages], refs[stages:]
    pool, refs = refs[:stages], refs[stages:]
    up_buf, refs = refs[:stages], refs[stages:]
    low_buf, refs = refs[:stages], refs[stages:]
    partial, refs = refs[:stages], refs[stages:]
    z_in, refs = refs[:stages], refs[stages:]
    z_sum, refs = refs[:stages], refs[stages:]
    y_in, refs = refs[:stages], refs[stages:]
    y_sum, refs = refs[:stages], refs[stages:]
    x_in, refs = refs[:stages], refs[stages:]
    (
        adj,
        grad_t,
        halves,
        up_rows,
        pre_rows,
        load_sem,
        adj_sem,
        row_sem,
        halo_send,
        halo_recv,
        core_send,
        core_recv,
        sum_send,
        sum_recv,
    ) = refs

    blocks = features.shape[0]
    hslice = upstream.shape[1]
    nodes = upstream.shape[0]
    row_steps = nodes // ROWS
    count = lax.axis_size("node")
    n, f = lax.axis_index("node"), lax.axis_index("feat")
    z, y, x = n // (SIDE * SIDE), (n // SIDE) % SIDE, n % SIDE
    upper, lower = lax.rem(n + 1, count), lax.rem(n + count - 1, count)

    def z_peer(d):
        return lax.rem(z + d, SIDE) * (SIDE * SIDE) + y * SIDE + x

    def y_peer(d):
        return z * (SIDE * SIDE) + lax.rem(y + d, SIDE) * SIDE + x

    def x_peer(d):
        return z * (SIDE * SIDE) + y * SIDE + lax.rem(x + d, SIDE)

    loads = []
    for k in range(stages):
        columns = features.at[:, :, pl.ds(k * COLS, COLS)]
        first = pltpu.make_async_copy(columns, own[k], load_sem.at[k, 0])
        second = pltpu.make_async_copy(columns, pool[k].at[pl.ds(cap, blocks)], load_sem.at[k, 1])
        first.start()
        loads.append((first, second))
    adj_load = pltpu.make_async_copy(adj_hbm, adj, adj_sem)

    def row_loads(step, slot):
        rows = pl.ds(pl.multiple_of(step * ROWS, ROWS), ROWS)
        return (
            pltpu.make_async_copy(upstream.at[rows], up_rows.at[slot], row_sem.at[slot, 0]),
            pltpu.make_async_copy(preact.at[rows], pre_rows.at[slot], row_sem.at[slot, 1]),
        )

    for copy in row_loads(0, 0):
        copy.start()
    adj_load.start()
    for k in range(stages):
        loads[k][1].start()

    barrier = pltpu.get_barrier_semaphore()
    greeted = [(upper, f), (lower, f), (n, 1 - f)]
    for d in range(1, SIDE):
        greeted += [(z_peer(d), f), (y_peer(d), f), (x_peer(d), f)]
    for target in greeted:
        pl.semaphore_signal(barrier, inc=1, device_id=target, device_id_type=MESH)

    def pack(k):
        loads[k][0].wait()

        def one(c, carry):
            up_buf[k][c] = own[k][to_upper[c]]
            low_buf[k][c] = own[k][to_lower[c]]
            return carry

        lax.fori_loop(0, cap, one, 0)

    def halo(k):
        return (
            pltpu.make_async_remote_copy(
                src_ref=up_buf[k],
                dst_ref=pool[k].at[pl.ds(0, cap)],
                send_sem=halo_send.at[k, 0],
                recv_sem=halo_recv.at[k, 0],
                device_id=(upper, f),
                device_id_type=MESH,
            ),
            pltpu.make_async_remote_copy(
                src_ref=low_buf[k],
                dst_ref=pool[k].at[pl.ds(cap + blocks, cap)],
                send_sem=halo_send.at[k, 1],
                recv_sem=halo_recv.at[k, 1],
                device_id=(lower, f),
                device_id_type=MESH,
            ),
        )

    halos = [halo(k) for k in range(stages)]
    pack(0)
    pl.semaphore_wait(barrier, len(greeted))
    for copy in halos[0]:
        copy.start()
    pack(1)
    for copy in halos[1]:
        copy.start()

    mine = pl.ds(pl.multiple_of(f * hslice, hslice), hslice)

    def core_copy(step):
        part = grad_t.at[mine, pl.ds(pl.multiple_of(step * ROWS, ROWS), ROWS)]
        return pltpu.make_async_remote_copy(
            src_ref=part,
            dst_ref=part,
            send_sem=core_send.at[step],
            recv_sem=core_recv.at[step],
            device_id=(n, 1 - f),
            device_id_type=MESH,
        )

    def mask_step(step, carry):
        slot = lax.rem(step, 2)

        @pl.when(step + 1 < row_steps)
        def _():
            for copy in row_loads(step + 1, 1 - slot):
                copy.start()

        for copy in row_loads(step, slot):
            copy.wait()
        kept = jnp.where(
            pre_rows[slot].astype(jnp.float32) > 0.0, up_rows[slot].astype(jnp.float32), 0.0
        )
        grad_t[mine, pl.ds(pl.multiple_of(step * ROWS, ROWS), ROWS)] = kept.astype(jnp.bfloat16).T
        core_copy(step).start()
        return carry

    lax.fori_loop(0, row_steps, mask_step, 0)
    adj_load.wait()
    for k in range(2, stages):
        pack(k)
    for k in range(stages):
        loads[k][1].wait()

    def core_wait(step, carry):
        core_copy(step).wait()
        return carry

    lax.fori_loop(0, row_steps, core_wait, 0)

    def sum_copy(k, phase, d, src, dst, target):
        return pltpu.make_async_remote_copy(
            src_ref=src,
            dst_ref=dst.at[d - 1],
            send_sem=sum_send.at[k, phase, d - 1],
            recv_sem=sum_recv.at[k, phase, d - 1],
            device_id=(target, f),
            device_id_type=MESH,
        )

    z_rows = partial[0].shape[0] // SIDE
    y_rows = z_rows // SIDE
    x_rows = y_rows // SIDE
    pending = []

    for k in range(stages):
        for copy in halos[k]:
            copy.wait_recv()
        if k + 2 < stages:
            for copy in halos[k + 2]:
                copy.start()

        def aggregate(b, carry):
            tiles = jnp.concatenate([adj[2 * b], adj[2 * b + 1]], axis=1)
            sources = jnp.concatenate([pool[k][where[2 * b]], pool[k][where[2 * b + 1]]], axis=0)
            total = jnp.dot(tiles, sources, preferred_element_type=jnp.float32)
            high = total.astype(jnp.bfloat16)
            low = (total - high.astype(jnp.float32)).astype(jnp.bfloat16)
            rows = pl.ds(pl.multiple_of(b * TILE, TILE), TILE)
            halves[rows, 0:COLS] = high
            halves[rows, COLS : 2 * COLS] = low
            return carry

        lax.fori_loop(0, blocks, aggregate, 0, unroll=4)

        z_copies = []
        for d in (2, 1, 3, 0):
            place = lax.rem(z + d, SIDE) * z_rows
            rows = pl.ds(pl.multiple_of(place, z_rows), z_rows)
            both = jnp.dot(grad_t[rows, :], halves[...], preferred_element_type=jnp.float32)
            partial[k][rows, :] = both[:, :COLS] + both[:, COLS:]
            if d:
                copy = sum_copy(k, 0, d, partial[k].at[rows], z_in[k], z_peer(d))
                copy.start()
                z_copies.append(copy)
        for copy in z_copies:
            copy.wait_recv()
        rows = pl.ds(pl.multiple_of(z * z_rows, z_rows), z_rows)
        z_sum[k][...] = partial[k][rows, :] + z_in[k][0] + z_in[k][1] + z_in[k][2]
        y_copies = []
        for d in (2, 1, 3):
            place = lax.rem(y + d, SIDE) * y_rows
            rows = pl.ds(pl.multiple_of(place, y_rows), y_rows)
            copy = sum_copy(k, 1, d, z_sum[k].at[rows], y_in[k], y_peer(d))
            copy.start()
            y_copies.append(copy)
        for copy in y_copies:
            copy.wait_recv()
        rows = pl.ds(pl.multiple_of(y * y_rows, y_rows), y_rows)
        y_sum[k][...] = z_sum[k][rows, :] + y_in[k][0] + y_in[k][1] + y_in[k][2]
        x_copies = []
        for d in (2, 1, 3):
            place = lax.rem(x + d, SIDE) * x_rows
            rows = pl.ds(pl.multiple_of(place, x_rows), x_rows)
            copy = sum_copy(k, 2, d, y_sum[k].at[rows], x_in[k], x_peer(d))
            copy.start()
            x_copies.append(copy)
        pending.append((z_copies + y_copies, x_copies))

    for k in range(stages):
        early, last = pending[k]
        for copy in last:
            copy.wait_recv()
        rows = pl.ds(pl.multiple_of(x * x_rows, x_rows), x_rows)
        out[:, k * COLS : (k + 1) * COLS] = y_sum[k][rows, :] + x_in[k][0] + x_in[k][1] + x_in[k][2]
        for copy in early + last:
            copy.wait_send()
        for copy in halos[k]:
            copy.wait_send()


def fused(cap, collective_id, features, upstream, preact, adj_tiles, where, to_upper, to_lower):
    nodes, fslice = features.shape
    hslice = upstream.shape[1]
    hidden = 2 * hslice
    blocks = nodes // TILE
    stages = fslice // COLS
    count = lax.axis_size("node")
    width = hidden // count
    f32, bf16 = jnp.float32, jnp.bfloat16

    def each(shape, dtype):
        return [pltpu.VMEM(shape, dtype)] * stages

    scratch = (
        each((blocks, TILE, COLS), bf16)
        + each((blocks + 2 * cap, TILE, COLS), bf16)
        + each((cap, TILE, COLS), bf16)
        + each((cap, TILE, COLS), bf16)
        + each((hidden, COLS), f32)
        + each((SIDE - 1, hidden // SIDE, COLS), f32)
        + each((hidden // SIDE, COLS), f32)
        + each((SIDE - 1, hidden // SIDE**2, COLS), f32)
        + each((hidden // SIDE**2, COLS), f32)
        + each((SIDE - 1, hidden // SIDE**3, COLS), f32)
        + [
            pltpu.VMEM(adj_tiles.shape, bf16),
            pltpu.VMEM((hidden, nodes), bf16),
            pltpu.VMEM((nodes, 2 * COLS), bf16),
            pltpu.VMEM((2, ROWS, hslice), bf16),
            pltpu.VMEM((2, ROWS, hslice), bf16),
            pltpu.SemaphoreType.DMA((stages, 2)),
            pltpu.SemaphoreType.DMA,
            pltpu.SemaphoreType.DMA((2, 2)),
            pltpu.SemaphoreType.DMA((stages, 2)),
            pltpu.SemaphoreType.DMA((stages, 2)),
            pltpu.SemaphoreType.DMA((nodes // ROWS,)),
            pltpu.SemaphoreType.DMA((nodes // ROWS,)),
            pltpu.SemaphoreType.DMA((stages, 3, SIDE - 1)),
            pltpu.SemaphoreType.DMA((stages, 3, SIDE - 1)),
        ]
    )
    in_hbm = pl.BlockSpec(memory_space=pl.ANY)
    in_smem = pl.BlockSpec(memory_space=pltpu.SMEM)
    flops = 4 * nodes * fslice * hidden + 4 * nodes * TILE * fslice
    return pl.pallas_call(
        functools.partial(fused_kernel, cap),
        out_shape=jax.ShapeDtypeStruct((width, fslice), f32),
        in_specs=[in_hbm] * 4 + [in_smem] * 3,
        out_specs=pl.BlockSpec(memory_space=pltpu.VMEM),
        scratch_shapes=scratch,
        cost_estimate=pl.CostEstimate(flops=flops, bytes_accessed=8 * nodes * fslice, transcendentals=0),
        compiler_params=pltpu.CompilerParams(
            collective_id=collective_id, has_side_effects=True, vmem_limit_bytes=62 * 1024 * 1024
        ),
    )(features.reshape(blocks, TILE, fslice), upstream, preact, adj_tiles, where, to_upper, to_lower)


def local(features, upstream, preact, adj_tiles, tile_source):
    nodes = features.shape[0]
    blocks = nodes // TILE
    factor = float(nodes * lax.axis_size("node")) ** (-0.5)
    order = jnp.arange(blocks, dtype=jnp.int32)
    summed = fused(blocks, 0, features, upstream, preact, adj_tiles, tile_source, order, order)
    return summed.T * factor


def solution(mesh):
    in_specs = (
        P("node", "feat"),
        P("node", "feat"),
        P("node", "feat"),
        P("node", None, None),
        P("node"),
    )
    out_specs = P("feat", "node")
    return jax.shard_map(local, mesh=mesh, in_specs=in_specs, out_specs=out_specs, check_vma=False)
```

```python
import functools

import jax
import jax.numpy as jnp
from jax import lax
from jax.experimental import pallas as pl
from jax.experimental.pallas import tpu as pltpu
from jax.sharding import PartitionSpec as P

MESH = pl.DeviceIdType.MESH
SIDE = 4
TILE = 128
COLS = 128
ROWS = 512
LANES = 128
CAPACITY = 28
PARTS = ((0, 0, 16, (0, 1, 2)), (1, 0, 16, (1, 2, 0)), (2, 0, 16, (2, 0, 1)), (3, 0, 8, (0, 1, 2)), (3, 8, 8, (1, 2, 0)))


def request(cap, blocks, sources):
    row = lax.broadcasted_iota(jnp.int32, (LANES, LANES), 0)
    column = lax.broadcasted_iota(jnp.int32, (LANES, LANES), 1)
    wide = jnp.broadcast_to(sources, (LANES, LANES))
    named = jnp.where(row == wide, 1, 0)
    used = jnp.max(jnp.where(column == wide.T, 1, 0), axis=0, keepdims=True)

    def group(index):
        return jnp.where(index >= blocks, 1, 0) + jnp.where(index >= 2 * blocks, 1, 0)

    before = jnp.logical_and(column < row, group(column) == group(row))
    rank = jnp.sum(jnp.where(before, used, 0), axis=1, keepdims=True)
    marked = jnp.max(named, axis=1, keepdims=True)
    chosen = jnp.where(rank == column, marked, 0)
    lower_rows = row < blocks
    upper_rows = row >= 2 * blocks
    from_lower = jnp.sum(jnp.where(lower_rows, chosen * row, 0), axis=0, keepdims=True)
    from_upper = jnp.sum(jnp.where(upper_rows, chosen * (row - 2 * blocks), 0), axis=0, keepdims=True)
    held = jnp.minimum(rank, cap - 1)
    target = jnp.where(lower_rows, held, jnp.where(upper_rows, held + (cap + blocks), row + (cap - blocks)))
    where = jnp.sum(named * target, axis=0, keepdims=True)
    lower_count = jnp.sum(jnp.where(lower_rows, marked, 0), axis=0, keepdims=True)
    upper_count = jnp.sum(jnp.where(upper_rows, marked, 0), axis=0, keepdims=True)
    over = jnp.where(jnp.maximum(lower_count, upper_count) > cap, 1.0, 0.0)
    return from_lower, from_upper, where, over


def within(index, size):
    return jnp.minimum(jnp.maximum(index, 0), size - 1)


def fused_kernel(cap, *refs):
    refs = list(refs)
    features, upstream, preact, adj_hbm, sources, out, over = refs[:7]
    refs = refs[7:]
    stages = features.shape[2] // COLS
    own, refs = refs[:stages], refs[stages:]
    pool, refs = refs[:stages], refs[stages:]
    up_buf, refs = refs[:stages], refs[stages:]
    low_buf, refs = refs[:stages], refs[stages:]
    partial, refs = refs[:stages], refs[stages:]
    sums, refs = refs[: 5 * len(PARTS)], refs[5 * len(PARTS) :]
    flag_in, refs = refs[:3], refs[3:]
    flag, refs = refs[:3], refs[3:]
    (
        ask_lower,
        ask_upper,
        asked_by_upper,
        asked_by_lower,
        found,
        to_upper,
        to_lower,
        where,
        adj,
        grad_t,
        halves,
        up_rows,
        pre_rows,
        load_sem,
        adj_sem,
        row_sem,
        list_send,
        list_recv,
        list_local,
        flag_send,
        flag_recv,
        halo_send,
        halo_recv,
        core_send,
        core_recv,
        sum_send,
        sum_recv,
    ) = refs

    blocks = features.shape[0]
    tiles = sources.shape[1]
    hslice = upstream.shape[1]
    nodes = upstream.shape[0]
    row_steps = nodes // ROWS
    count = lax.axis_size("node")
    n, f = lax.axis_index("node"), lax.axis_index("feat")
    z, y, x = n // (SIDE * SIDE), (n // SIDE) % SIDE, n % SIDE
    upper, lower = lax.rem(n + 1, count), lax.rem(n + count - 1, count)

    def z_peer(d):
        return lax.rem(z + d, SIDE) * (SIDE * SIDE) + y * SIDE + x

    def y_peer(d):
        return z * (SIDE * SIDE) + lax.rem(y + d, SIDE) * SIDE + x

    def x_peer(d):
        return z * (SIDE * SIDE) + y * SIDE + lax.rem(x + d, SIDE)

    def remote(src, dst, send, recv, target):
        return pltpu.make_async_remote_copy(
            src_ref=src, dst_ref=dst, send_sem=send, recv_sem=recv, device_id=target, device_id_type=MESH
        )

    columns = [features.at[:, :, pl.ds(k * COLS, COLS)] for k in range(stages)]
    own_load = [pltpu.make_async_copy(columns[k], own[k], load_sem.at[k, 0]) for k in range(stages)]
    pool_load = [
        pltpu.make_async_copy(columns[k], pool[k].at[pl.ds(cap, blocks)], load_sem.at[k, 1]) for k in range(stages)
    ]
    adj_load = pltpu.make_async_copy(adj_hbm, adj, adj_sem)

    def row_loads(step, slot):
        rows = pl.ds(pl.multiple_of(step * ROWS, ROWS), ROWS)
        return (
            pltpu.make_async_copy(upstream.at[rows], up_rows.at[slot], row_sem.at[slot, 0]),
            pltpu.make_async_copy(preact.at[rows], pre_rows.at[slot], row_sem.at[slot, 1]),
        )

    own_load[0].start()
    own_load[1].start()
    for copy in row_loads(0, 0):
        copy.start()
    barrier = pltpu.get_barrier_semaphore()
    greeted = [(upper, f), (lower, f), (n, 1 - f)]
    for d in range(1, SIDE):
        greeted += [(z_peer(d), f), (y_peer(d), f), (x_peer(d), f)]
    for target in greeted:
        pl.semaphore_signal(barrier, inc=1, device_id=target, device_id_type=MESH)

    found[...] = jnp.full(found.shape, -1, jnp.int32)
    found[0:1, 0:tiles] = sources[...]
    from_lower, from_upper, spots, excess = request(cap, blocks, found[0:1, :])
    ask_lower[...] = jnp.broadcast_to(from_lower, ask_lower.shape)
    ask_upper[...] = jnp.broadcast_to(from_upper, ask_upper.shape)
    found[...] = jnp.broadcast_to(spots, found.shape)
    flag[0][...] = jnp.broadcast_to(excess, flag[0].shape)

    pl.semaphore_wait(barrier, len(greeted))
    ask = (
        remote(ask_lower, asked_by_upper, list_send.at[0], list_recv.at[0], (lower, f)),
        remote(ask_upper, asked_by_lower, list_send.at[1], list_recv.at[1], (upper, f)),
    )
    for copy in ask:
        copy.start()
    place_local = pltpu.make_async_copy(found, where, list_local.at[2])
    place_local.start()

    peers = (z_peer, y_peer, x_peer)
    position = (z, y, x)
    flags = [
        [
            remote(
                flag[phase],
                flag_in[phase].at[d - 1],
                flag_send.at[phase, d - 1],
                flag_recv.at[phase, d - 1],
                (peers[phase](d), f),
            )
            for d in range(1, SIDE)
        ]
        for phase in range(3)
    ]

    def flag_total(phase):
        for copy in flags[phase]:
            copy.wait_recv()
        return flag[phase][...] + flag_in[phase][0] + flag_in[phase][1] + flag_in[phase][2]

    ask[0].wait_recv()
    local_upper = pltpu.make_async_copy(asked_by_upper, to_upper, list_local.at[0])
    local_upper.start()
    ask[1].wait_recv()
    local_lower = pltpu.make_async_copy(asked_by_lower, to_lower, list_local.at[1])
    local_lower.start()
    local_upper.wait()
    local_lower.wait()

    halos = [
        (
            remote(up_buf[k], pool[k].at[pl.ds(0, cap)], halo_send.at[k, 0], halo_recv.at[k, 0], (upper, f)),
            remote(low_buf[k], pool[k].at[pl.ds(cap + blocks, cap)], halo_send.at[k, 1], halo_recv.at[k, 1], (lower, f)),
        )
        for k in range(stages)
    ]

    def pack(k):
        own_load[k].wait()

        def one(c, carry):
            up_buf[k][c] = own[k][within(to_upper[0, c], blocks)]
            low_buf[k][c] = own[k][within(to_lower[0, c], blocks)]
            return carry

        lax.fori_loop(0, cap, one, 0, unroll=2)

    for k in range(stages):
        pack(k)
        for copy in halos[k]:
            copy.start()
        if k == 0:
            for later in range(2, stages):
                own_load[later].start()
    adj_load.start()
    for k in range(stages):
        pool_load[k].start()

    mine = pl.ds(pl.multiple_of(f * hslice, hslice), hslice)

    def core_copy(step):
        part = grad_t.at[mine, pl.ds(pl.multiple_of(step * ROWS, ROWS), ROWS)]
        return remote(part, part, core_send.at[step], core_recv.at[step], (n, 1 - f))

    def mask_step(step, carry):
        slot = lax.rem(step, 2)

        @pl.when(step + 1 < row_steps)
        def _():
            for copy in row_loads(step + 1, 1 - slot):
                copy.start()

        for copy in row_loads(step, slot):
            copy.wait()
        kept = jnp.where(pre_rows[slot].astype(jnp.float32) > 0.0, up_rows[slot].astype(jnp.float32), 0.0)
        grad_t[mine, pl.ds(pl.multiple_of(step * ROWS, ROWS), ROWS)] = kept.astype(jnp.bfloat16).T
        core_copy(step).start()
        return carry

    lax.fori_loop(0, row_steps, mask_step, 0)
    adj_load.wait()
    for k in range(stages):
        pool_load[k].wait()

    def core_wait(step, carry):
        core_copy(step).wait()
        return carry

    lax.fori_loop(0, row_steps, core_wait, 0)
    place_local.wait()

    sent = []

    def buffers(i):
        first_in, first_sum, second_in, second_sum, third_in = sums[5 * i : 5 * i + 5]
        return (first_in, second_in, third_in), (None, first_sum, second_sum)

    def source(i, phase, place):
        stage, low, rows, order = PARTS[i]
        if phase == 0:
            spot = [slice(None)] * 3
            spot[order[0]] = place
            return partial[stage], tuple(spot) + (pl.ds(low, rows),)
        held = buffers(i)[1][phase]
        if phase == 1 and order[1] == max(order[1:]):
            return held, (slice(None), place)
        return held, (place,)

    arriving = {}

    def send(i, phase):
        axis = PARTS[i][3][phase]
        arriving[i] = []
        for d in (2, 1, 3):
            ref, spot = source(i, phase, lax.rem(position[axis] + d, SIDE))
            copy = remote(
                ref.at[spot],
                buffers(i)[0][phase].at[d - 1],
                sum_send.at[i, phase, d - 1],
                sum_recv.at[i, phase, d - 1],
                (peers[axis](d), f),
            )
            copy.start()
            arriving[i].append(copy)
        sent.extend(arriving[i])

    def total(i, phase):
        for copy in arriving[i]:
            copy.wait_recv()
        ref, spot = source(i, phase, position[PARTS[i][3][phase]])
        got = buffers(i)[0][phase]
        return ref[spot] + got[0] + got[1] + got[2]

    z_shape = partial[0].shape[1:]
    z_rows = z_shape[0] * z_shape[1] * z_shape[2]

    def multiply(k):
        def one(place, carry):
            rows = pl.ds(pl.multiple_of(place * z_rows, z_rows), z_rows)
            both = jnp.dot(grad_t[rows, :], halves[...], preferred_element_type=jnp.float32)
            partial[k][place] = (both[:, :COLS] + both[:, COLS:]).reshape(z_shape)
            return carry

        lax.fori_loop(0, SIDE, one, 0)

    for k in range(stages):
        for copy in halos[k]:
            copy.wait_recv()
        if k == stages - 1:
            for i in range(len(PARTS)):
                if PARTS[i][0] != k:
                    send(i, 0)
            for copy in flags[0]:
                copy.start()

        def aggregate(b, carry):
            pair = jnp.concatenate([adj[2 * b], adj[2 * b + 1]], axis=1)
            left = within(where[0, 2 * b], blocks + 2 * cap)
            right = within(where[0, 2 * b + 1], blocks + 2 * cap)
            inputs = jnp.concatenate([pool[k][left], pool[k][right]], axis=0)
            total = jnp.dot(pair, inputs, preferred_element_type=jnp.float32)
            high = total.astype(jnp.bfloat16)
            low = (total - high.astype(jnp.float32)).astype(jnp.bfloat16)
            rows = pl.ds(pl.multiple_of(b * TILE, TILE), TILE)
            halves[rows, 0:COLS] = high
            halves[rows, COLS : 2 * COLS] = low
            return carry

        lax.fori_loop(0, blocks, aggregate, 0, unroll=4)
        multiply(k)
    for i in range(len(PARTS)):
        if PARTS[i][0] == stages - 1:
            send(i, 0)
    for phase in (1, 2):
        for i in range(len(PARTS)):
            buffers(i)[1][phase][...] = total(i, phase - 1)
            send(i, phase)
        flag[phase][...] = flag_total(phase - 1)
        for copy in flags[phase]:
            copy.start()
    for i in range(len(PARTS)):
        stage, low, rows, _ = PARTS[i]
        out[low : low + rows, stage * COLS : (stage + 1) * COLS] = total(i, 2)
    over[...] = flag_total(2)
    for copy in sent:
        copy.wait_send()
    for pair in halos + [ask] + flags:
        for copy in pair:
            copy.wait_send()


def fused(cap, collective_id, features, upstream, preact, adj_tiles, sources):
    nodes, fslice = features.shape
    hslice = upstream.shape[1]
    hidden = 2 * hslice
    blocks = nodes // TILE
    stages = fslice // COLS
    width = hidden // lax.axis_size("node")
    f32, bf16, i32 = jnp.float32, jnp.bfloat16, jnp.int32
    peers = SIDE - 1
    steps = nodes // ROWS

    def each(shape, dtype, times=stages):
        return [pltpu.VMEM(shape, dtype)] * times

    def sems(*shape):
        return pltpu.SemaphoreType.DMA(shape)

    sums = []
    for _, _, rows, _ in PARTS:
        sums += [
            pltpu.VMEM((peers, SIDE, SIDE, rows, COLS), f32),
            pltpu.VMEM((SIDE, SIDE, rows, COLS), f32),
            pltpu.VMEM((peers, SIDE, rows, COLS), f32),
            pltpu.VMEM((SIDE, rows, COLS), f32),
            pltpu.VMEM((peers, rows, COLS), f32),
        ]

    scratch = (
        each((blocks, TILE, COLS), bf16)
        + each((blocks + 2 * cap, TILE, COLS), bf16)
        + each((cap, TILE, COLS), bf16)
        + each((cap, TILE, COLS), bf16)
        + each((SIDE, SIDE, SIDE, width, COLS), f32)
        + sums
        + each((peers, 8, LANES), f32, 3)
        + each((8, LANES), f32, 3)
        + each((8, LANES), i32, 5)
        + [pltpu.SMEM((8, LANES), i32)] * 3
        + [
            pltpu.VMEM(adj_tiles.shape, bf16),
            pltpu.VMEM((hidden, nodes), bf16),
            pltpu.VMEM((nodes, 2 * COLS), bf16),
            pltpu.VMEM((2, ROWS, hslice), bf16),
            pltpu.VMEM((2, ROWS, hslice), bf16),
            sems(stages, 2),
            pltpu.SemaphoreType.DMA,
            sems(2, 2),
            sems(2),
            sems(2),
            sems(3),
            sems(3, peers),
            sems(3, peers),
            sems(stages, 2),
            sems(stages, 2),
            sems(steps),
            sems(steps),
            sems(len(PARTS), 3, peers),
            sems(len(PARTS), 3, peers),
        ]
    )
    in_hbm = pl.BlockSpec(memory_space=pl.ANY)
    in_vmem = pl.BlockSpec(memory_space=pltpu.VMEM)
    flops = 4 * nodes * fslice * hidden + 4 * nodes * TILE * fslice
    return pl.pallas_call(
        functools.partial(fused_kernel, cap),
        out_shape=(jax.ShapeDtypeStruct((width, fslice), f32), jax.ShapeDtypeStruct((8, LANES), f32)),
        in_specs=[in_hbm] * 4 + [in_vmem],
        out_specs=(in_vmem, in_vmem),
        scratch_shapes=scratch,
        cost_estimate=pl.CostEstimate(flops=flops, bytes_accessed=8 * nodes * fslice, transcendentals=0),
        compiler_params=pltpu.CompilerParams(
            collective_id=collective_id, has_side_effects=True, vmem_limit_bytes=62 * 1024 * 1024
        ),
    )(features.reshape(blocks, TILE, fslice), upstream, preact, adj_tiles, sources)


def local(features, upstream, preact, adj_tiles, tile_source):
    nodes = features.shape[0]
    blocks = nodes // TILE
    factor = float(nodes * lax.axis_size("node")) ** (-0.5)
    args = (features, upstream, preact, adj_tiles, tile_source.reshape(1, -1))
    summed, over = fused(CAPACITY, 0, *args)
    summed = lax.cond(over[0, 0] > 0.0, lambda: fused(blocks, 1, *args)[0], lambda: summed)
    return summed.T * factor


def solution(mesh):
    in_specs = (
        P("node", "feat"),
        P("node", "feat"),
        P("node", "feat"),
        P("node", None, None),
        P("node"),
    )
    out_specs = P("feat", "node")
    return jax.shard_map(local, mesh=mesh, in_specs=in_specs, out_specs=out_specs, check_vma=False)
```

```python
import functools

import jax
import jax.numpy as jnp
from jax import lax
from jax.experimental import pallas as pl
from jax.experimental.pallas import tpu as pltpu
from jax.sharding import PartitionSpec as P

MESH = pl.DeviceIdType.MESH
SIDE = 4
TILE = 128
COLS = 128
ROWS = 512
LANES = 128
CAPACITY = 28
PARTS = ((0, 0, 16, (0, 1, 2)), (1, 0, 16, (1, 2, 0)), (2, 0, 16, (2, 0, 1)), (3, 0, 8, (0, 1, 2)), (3, 8, 8, (1, 2, 0)))


def request(skip, cap, blocks, sources):
    row = lax.broadcasted_iota(jnp.int32, (LANES, LANES), 0)
    column = lax.broadcasted_iota(jnp.int32, (LANES, LANES), 1)
    wide = jnp.broadcast_to(sources, (LANES, LANES))
    named = jnp.where(row == wide, 1, 0)
    used = jnp.max(jnp.where(column == wide.T, 1, 0), axis=0, keepdims=True)

    def group(index):
        return jnp.where(index >= blocks, 1, 0) + jnp.where(index >= 2 * blocks, 1, 0)

    before = jnp.logical_and(column < row, group(column) == group(row))
    rank = jnp.sum(jnp.where(before, used, 0), axis=1, keepdims=True)
    marked = jnp.max(named, axis=1, keepdims=True)
    chosen = jnp.where(rank == column + skip, marked, 0)
    lower_rows = row < blocks
    upper_rows = row >= 2 * blocks
    from_lower = jnp.sum(jnp.where(lower_rows, chosen * row, 0), axis=0, keepdims=True)
    from_upper = jnp.sum(jnp.where(upper_rows, chosen * (row - 2 * blocks), 0), axis=0, keepdims=True)
    nothing = blocks + 2 * cap
    slot = rank - skip
    here = jnp.logical_and(slot >= 0, slot < cap)
    lower_place = jnp.where(here, slot, nothing)
    upper_place = jnp.where(here, slot + (cap + blocks), nothing)
    own_place = nothing + 0 * row if skip else row + (cap - blocks)
    target = jnp.where(lower_rows, lower_place, jnp.where(upper_rows, upper_place, own_place))
    where = jnp.sum(named * target, axis=0, keepdims=True)
    lower_count = jnp.sum(jnp.where(lower_rows, marked, 0), axis=0, keepdims=True)
    upper_count = jnp.sum(jnp.where(upper_rows, marked, 0), axis=0, keepdims=True)
    over = jnp.where(jnp.maximum(lower_count, upper_count) > skip + cap, 1.0, 0.0)
    return from_lower, from_upper, where, over


def within(index, size):
    return jnp.minimum(jnp.maximum(index, 0), size - 1)


def fused_kernel(skip, cap, *refs):
    refs = list(refs)
    features, upstream, preact, adj_hbm, sources, out, over = refs[:7]
    refs = refs[7:]
    stages = features.shape[2] // COLS
    own, refs = refs[:stages], refs[stages:]
    pool, refs = refs[:stages], refs[stages:]
    up_buf, refs = refs[:stages], refs[stages:]
    low_buf, refs = refs[:stages], refs[stages:]
    partial, refs = refs[:stages], refs[stages:]
    sums, refs = refs[: 5 * len(PARTS)], refs[5 * len(PARTS) :]
    flag_in, refs = refs[:3], refs[3:]
    flag, refs = refs[:3], refs[3:]
    (
        ask_lower,
        ask_upper,
        asked_by_upper,
        asked_by_lower,
        found,
        to_upper,
        to_lower,
        where,
        adj,
        grad_t,
        halves,
        up_rows,
        pre_rows,
        load_sem,
        adj_sem,
        row_sem,
        list_send,
        list_recv,
        list_local,
        flag_send,
        flag_recv,
        halo_send,
        halo_recv,
        core_send,
        core_recv,
        sum_send,
        sum_recv,
    ) = refs

    blocks = features.shape[0]
    tiles = sources.shape[1]
    hslice = upstream.shape[1]
    nodes = upstream.shape[0]
    row_steps = nodes // ROWS
    count = lax.axis_size("node")
    n, f = lax.axis_index("node"), lax.axis_index("feat")
    z, y, x = n // (SIDE * SIDE), (n // SIDE) % SIDE, n % SIDE
    upper, lower = lax.rem(n + 1, count), lax.rem(n + count - 1, count)

    def z_peer(d):
        return lax.rem(z + d, SIDE) * (SIDE * SIDE) + y * SIDE + x

    def y_peer(d):
        return z * (SIDE * SIDE) + lax.rem(y + d, SIDE) * SIDE + x

    def x_peer(d):
        return z * (SIDE * SIDE) + y * SIDE + lax.rem(x + d, SIDE)

    def remote(src, dst, send, recv, target):
        return pltpu.make_async_remote_copy(
            src_ref=src, dst_ref=dst, send_sem=send, recv_sem=recv, device_id=target, device_id_type=MESH
        )

    columns = [features.at[:, :, pl.ds(k * COLS, COLS)] for k in range(stages)]
    own_load = [pltpu.make_async_copy(columns[k], own[k], load_sem.at[k, 0]) for k in range(stages)]
    pool_load = [
        pltpu.make_async_copy(columns[k], pool[k].at[pl.ds(cap, blocks)], load_sem.at[k, 1]) for k in range(stages)
    ]
    adj_load = pltpu.make_async_copy(adj_hbm, adj, adj_sem)

    def row_loads(step, slot):
        rows = pl.ds(pl.multiple_of(step * ROWS, ROWS), ROWS)
        return (
            pltpu.make_async_copy(upstream.at[rows], up_rows.at[slot], row_sem.at[slot, 0]),
            pltpu.make_async_copy(preact.at[rows], pre_rows.at[slot], row_sem.at[slot, 1]),
        )

    own_load[0].start()
    own_load[1].start()
    for copy in row_loads(0, 0):
        copy.start()
    barrier = pltpu.get_barrier_semaphore()
    greeted = [(upper, f), (lower, f), (n, 1 - f)]
    for d in range(1, SIDE):
        greeted += [(z_peer(d), f), (y_peer(d), f), (x_peer(d), f)]
    for target in greeted:
        pl.semaphore_signal(barrier, inc=1, device_id=target, device_id_type=MESH)

    found[...] = jnp.full(found.shape, -1, jnp.int32)
    found[0:1, 0:tiles] = sources[...]
    from_lower, from_upper, spots, excess = request(skip, cap, blocks, found[0:1, :])
    ask_lower[...] = jnp.broadcast_to(from_lower, ask_lower.shape)
    ask_upper[...] = jnp.broadcast_to(from_upper, ask_upper.shape)
    found[...] = jnp.broadcast_to(spots, found.shape)
    flag[0][...] = jnp.broadcast_to(excess, flag[0].shape)

    pl.semaphore_wait(barrier, len(greeted))
    ask = (
        remote(ask_lower, asked_by_upper, list_send.at[0], list_recv.at[0], (lower, f)),
        remote(ask_upper, asked_by_lower, list_send.at[1], list_recv.at[1], (upper, f)),
    )
    for copy in ask:
        copy.start()
    place_local = pltpu.make_async_copy(found, where, list_local.at[2])
    place_local.start()

    peers = (z_peer, y_peer, x_peer)
    position = (z, y, x)
    flags = [
        [
            remote(
                flag[phase],
                flag_in[phase].at[d - 1],
                flag_send.at[phase, d - 1],
                flag_recv.at[phase, d - 1],
                (peers[phase](d), f),
            )
            for d in range(1, SIDE)
        ]
        for phase in range(3)
    ]

    def flag_total(phase):
        for copy in flags[phase]:
            copy.wait_recv()
        return flag[phase][...] + flag_in[phase][0] + flag_in[phase][1] + flag_in[phase][2]

    ask[0].wait_recv()
    local_upper = pltpu.make_async_copy(asked_by_upper, to_upper, list_local.at[0])
    local_upper.start()
    ask[1].wait_recv()
    local_lower = pltpu.make_async_copy(asked_by_lower, to_lower, list_local.at[1])
    local_lower.start()
    local_upper.wait()
    local_lower.wait()

    halos = [
        (
            remote(up_buf[k], pool[k].at[pl.ds(0, cap)], halo_send.at[k, 0], halo_recv.at[k, 0], (upper, f)),
            remote(low_buf[k], pool[k].at[pl.ds(cap + blocks, cap)], halo_send.at[k, 1], halo_recv.at[k, 1], (lower, f)),
        )
        for k in range(stages)
    ]

    def pack(k):
        own_load[k].wait()

        def one(c, carry):
            up_buf[k][c] = own[k][within(to_upper[0, c], blocks)]
            low_buf[k][c] = own[k][within(to_lower[0, c], blocks)]
            return carry

        lax.fori_loop(0, cap, one, 0, unroll=2)

    for k in range(stages):
        pack(k)
        for copy in halos[k]:
            copy.start()
        if k == 0:
            for later in range(2, stages):
                own_load[later].start()
    adj_load.start()
    for k in range(stages):
        pool_load[k].start()
        pool[k][blocks + 2 * cap] = jnp.zeros((TILE, COLS), jnp.bfloat16)

    mine = pl.ds(pl.multiple_of(f * hslice, hslice), hslice)

    def core_copy(step):
        part = grad_t.at[mine, pl.ds(pl.multiple_of(step * ROWS, ROWS), ROWS)]
        return remote(part, part, core_send.at[step], core_recv.at[step], (n, 1 - f))

    def mask_step(step, carry):
        slot = lax.rem(step, 2)

        @pl.when(step + 1 < row_steps)
        def _():
            for copy in row_loads(step + 1, 1 - slot):
                copy.start()

        for copy in row_loads(step, slot):
            copy.wait()
        kept = jnp.where(pre_rows[slot].astype(jnp.float32) > 0.0, up_rows[slot].astype(jnp.float32), 0.0)
        grad_t[mine, pl.ds(pl.multiple_of(step * ROWS, ROWS), ROWS)] = kept.astype(jnp.bfloat16).T
        core_copy(step).start()
        return carry

    lax.fori_loop(0, row_steps, mask_step, 0)
    adj_load.wait()
    for k in range(stages):
        pool_load[k].wait()

    def core_wait(step, carry):
        core_copy(step).wait()
        return carry

    lax.fori_loop(0, row_steps, core_wait, 0)
    place_local.wait()

    sent = []

    def buffers(i):
        first_in, first_sum, second_in, second_sum, third_in = sums[5 * i : 5 * i + 5]
        return (first_in, second_in, third_in), (None, first_sum, second_sum)

    def source(i, phase, place):
        stage, low, rows, order = PARTS[i]
        if phase == 0:
            spot = [slice(None)] * 3
            spot[order[0]] = place
            return partial[stage], tuple(spot) + (pl.ds(low, rows),)
        held = buffers(i)[1][phase]
        if phase == 1 and order[1] == max(order[1:]):
            return held, (slice(None), place)
        return held, (place,)

    arriving = {}

    def send(i, phase):
        axis = PARTS[i][3][phase]
        arriving[i] = []
        for d in (2, 1, 3):
            ref, spot = source(i, phase, lax.rem(position[axis] + d, SIDE))
            copy = remote(
                ref.at[spot],
                buffers(i)[0][phase].at[d - 1],
                sum_send.at[i, phase, d - 1],
                sum_recv.at[i, phase, d - 1],
                (peers[axis](d), f),
            )
            copy.start()
            arriving[i].append(copy)
        sent.extend(arriving[i])

    def total(i, phase):
        for copy in arriving[i]:
            copy.wait_recv()
        ref, spot = source(i, phase, position[PARTS[i][3][phase]])
        got = buffers(i)[0][phase]
        return ref[spot] + got[0] + got[1] + got[2]

    z_shape = partial[0].shape[1:]
    z_rows = z_shape[0] * z_shape[1] * z_shape[2]

    def multiply(k):
        def one(place, carry):
            rows = pl.ds(pl.multiple_of(place * z_rows, z_rows), z_rows)
            both = jnp.dot(grad_t[rows, :], halves[...], preferred_element_type=jnp.float32)
            partial[k][place] = (both[:, :COLS] + both[:, COLS:]).reshape(z_shape)
            return carry

        lax.fori_loop(0, SIDE, one, 0)

    for k in range(stages):
        for copy in halos[k]:
            copy.wait_recv()
        if k == stages - 1:
            for i in range(len(PARTS)):
                if PARTS[i][0] != k:
                    send(i, 0)
            for copy in flags[0]:
                copy.start()

        def aggregate(b, carry):
            pair = jnp.concatenate([adj[2 * b], adj[2 * b + 1]], axis=1)
            left = within(where[0, 2 * b], blocks + 2 * cap + 1)
            right = within(where[0, 2 * b + 1], blocks + 2 * cap + 1)
            inputs = jnp.concatenate([pool[k][left], pool[k][right]], axis=0)
            total = jnp.dot(pair, inputs, preferred_element_type=jnp.float32)
            high = total.astype(jnp.bfloat16)
            low = (total - high.astype(jnp.float32)).astype(jnp.bfloat16)
            rows = pl.ds(pl.multiple_of(b * TILE, TILE), TILE)
            halves[rows, 0:COLS] = high
            halves[rows, COLS : 2 * COLS] = low
            return carry

        lax.fori_loop(0, blocks, aggregate, 0, unroll=8)
        multiply(k)
    for i in range(len(PARTS)):
        if PARTS[i][0] == stages - 1:
            send(i, 0)
    for phase in (1, 2):
        for i in range(len(PARTS)):
            buffers(i)[1][phase][...] = total(i, phase - 1)
            send(i, phase)
        flag[phase][...] = flag_total(phase - 1)
        for copy in flags[phase]:
            copy.start()
    for i in range(len(PARTS)):
        stage, low, rows, _ = PARTS[i]
        out[low : low + rows, stage * COLS : (stage + 1) * COLS] = total(i, 2)
    over[...] = flag_total(2)
    for copy in sent:
        copy.wait_send()
    for pair in halos + [ask] + flags:
        for copy in pair:
            copy.wait_send()


def fused(skip, cap, collective_id, features, upstream, preact, adj_tiles, sources):
    nodes, fslice = features.shape
    hslice = upstream.shape[1]
    hidden = 2 * hslice
    blocks = nodes // TILE
    stages = fslice // COLS
    width = hidden // lax.axis_size("node")
    f32, bf16, i32 = jnp.float32, jnp.bfloat16, jnp.int32
    peers = SIDE - 1
    steps = nodes // ROWS

    def each(shape, dtype, times=stages):
        return [pltpu.VMEM(shape, dtype)] * times

    def sems(*shape):
        return pltpu.SemaphoreType.DMA(shape)

    sums = []
    for _, _, rows, _ in PARTS:
        sums += [
            pltpu.VMEM((peers, SIDE, SIDE, rows, COLS), f32),
            pltpu.VMEM((SIDE, SIDE, rows, COLS), f32),
            pltpu.VMEM((peers, SIDE, rows, COLS), f32),
            pltpu.VMEM((SIDE, rows, COLS), f32),
            pltpu.VMEM((peers, rows, COLS), f32),
        ]

    scratch = (
        each((blocks, TILE, COLS), bf16)
        + each((blocks + 2 * cap + 1, TILE, COLS), bf16)
        + each((cap, TILE, COLS), bf16)
        + each((cap, TILE, COLS), bf16)
        + each((SIDE, SIDE, SIDE, width, COLS), f32)
        + sums
        + each((peers, 8, LANES), f32, 3)
        + each((8, LANES), f32, 3)
        + each((8, LANES), i32, 5)
        + [pltpu.SMEM((8, LANES), i32)] * 3
        + [
            pltpu.VMEM(adj_tiles.shape, bf16),
            pltpu.VMEM((hidden, nodes), bf16),
            pltpu.VMEM((nodes, 2 * COLS), bf16),
            pltpu.VMEM((2, ROWS, hslice), bf16),
            pltpu.VMEM((2, ROWS, hslice), bf16),
            sems(stages, 2),
            pltpu.SemaphoreType.DMA,
            sems(2, 2),
            sems(2),
            sems(2),
            sems(3),
            sems(3, peers),
            sems(3, peers),
            sems(stages, 2),
            sems(stages, 2),
            sems(steps),
            sems(steps),
            sems(len(PARTS), 3, peers),
            sems(len(PARTS), 3, peers),
        ]
    )
    in_hbm = pl.BlockSpec(memory_space=pl.ANY)
    in_vmem = pl.BlockSpec(memory_space=pltpu.VMEM)
    flops = 4 * nodes * fslice * hidden + 4 * nodes * TILE * fslice
    return pl.pallas_call(
        functools.partial(fused_kernel, skip, cap),
        out_shape=(jax.ShapeDtypeStruct((width, fslice), f32), jax.ShapeDtypeStruct((8, LANES), f32)),
        in_specs=[in_hbm] * 4 + [in_vmem],
        out_specs=(in_vmem, in_vmem),
        scratch_shapes=scratch,
        cost_estimate=pl.CostEstimate(flops=flops, bytes_accessed=8 * nodes * fslice, transcendentals=0),
        compiler_params=pltpu.CompilerParams(
            collective_id=collective_id, has_side_effects=True, vmem_limit_bytes=62 * 1024 * 1024
        ),
    )(features.reshape(blocks, TILE, fslice), upstream, preact, adj_tiles, sources)


def local(features, upstream, preact, adj_tiles, tile_source):
    nodes = features.shape[0]
    blocks = nodes // TILE
    factor = float(nodes * lax.axis_size("node")) ** (-0.5)
    args = (features, upstream, preact, adj_tiles, tile_source.reshape(1, -1))
    summed, over = fused(0, CAPACITY, 0, *args)
    summed = lax.cond(
        over[0, 0] > 0.0, lambda: summed + fused(CAPACITY, blocks - CAPACITY, 1, *args)[0], lambda: summed
    )
    return summed.T * factor


def solution(mesh):
    in_specs = (
        P("node", "feat"),
        P("node", "feat"),
        P("node", "feat"),
        P("node", None, None),
        P("node"),
    )
    out_specs = P("feat", "node")
    return jax.shard_map(local, mesh=mesh, in_specs=in_specs, out_specs=out_specs, check_vma=False)
```

```python
import functools

import jax
import jax.numpy as jnp
from jax import lax
from jax.experimental import pallas as pl
from jax.experimental.pallas import tpu as pltpu
from jax.sharding import PartitionSpec as P

MESH = pl.DeviceIdType.MESH
SIDE = 4
TILE = 128
COLS = 128
ROWS = 512
LANES = 128
CAPACITY = 28
PARTS = ((0, 0, 16, (0, 1, 2)), (1, 0, 16, (1, 2, 0)), (2, 0, 16, (2, 0, 1)), (3, 0, 8, (0, 1, 2)), (3, 8, 8, (1, 2, 0)))


def request(skip, cap, blocks, sources):
    row = lax.broadcasted_iota(jnp.int32, (LANES, LANES), 0)
    column = lax.broadcasted_iota(jnp.int32, (LANES, LANES), 1)
    wide = jnp.broadcast_to(sources, (LANES, LANES))
    named = jnp.where(row == wide, 1, 0)
    used = jnp.max(jnp.where(column == wide.T, 1, 0), axis=0, keepdims=True)

    def group(index):
        return jnp.where(index >= blocks, 1, 0) + jnp.where(index >= 2 * blocks, 1, 0)

    before = jnp.logical_and(column < row, group(column) == group(row))
    rank = jnp.sum(jnp.where(before, used, 0), axis=1, keepdims=True)
    marked = jnp.max(named, axis=1, keepdims=True)
    chosen = jnp.where(rank == column + skip, marked, 0)
    lower_rows = row < blocks
    upper_rows = row >= 2 * blocks
    from_lower = jnp.sum(jnp.where(lower_rows, chosen * row, 0), axis=0, keepdims=True)
    from_upper = jnp.sum(jnp.where(upper_rows, chosen * (row - 2 * blocks), 0), axis=0, keepdims=True)
    nothing = blocks + 2 * cap
    slot = rank - skip
    here = jnp.logical_and(slot >= 0, slot < cap)
    lower_place = jnp.where(here, slot, nothing)
    upper_place = jnp.where(here, slot + (cap + blocks), nothing)
    own_place = nothing + 0 * row if skip else row + (cap - blocks)
    target = jnp.where(lower_rows, lower_place, jnp.where(upper_rows, upper_place, own_place))
    where = jnp.sum(named * target, axis=0, keepdims=True)
    lower_count = jnp.sum(jnp.where(lower_rows, marked, 0), axis=0, keepdims=True)
    upper_count = jnp.sum(jnp.where(upper_rows, marked, 0), axis=0, keepdims=True)
    over = jnp.where(jnp.maximum(lower_count, upper_count) > skip + cap, 1.0, 0.0)
    return from_lower, from_upper, where, over


def within(index, size):
    return jnp.minimum(jnp.maximum(index, 0), size - 1)


def fused_kernel(skip, cap, *refs):
    refs = list(refs)
    features, upstream, preact, adj_hbm, sources, out, over = refs[:7]
    refs = refs[7:]
    stages = features.shape[2] // COLS
    own, refs = refs[:stages], refs[stages:]
    pool, refs = refs[:stages], refs[stages:]
    up_buf, refs = refs[:stages], refs[stages:]
    low_buf, refs = refs[:stages], refs[stages:]
    partial, refs = refs[:stages], refs[stages:]
    sums, refs = refs[: 5 * len(PARTS)], refs[5 * len(PARTS) :]
    flag_in, refs = refs[:3], refs[3:]
    flag, refs = refs[:3], refs[3:]
    (
        ask_lower,
        ask_upper,
        asked_by_upper,
        asked_by_lower,
        found,
        to_upper,
        to_lower,
        where,
        adj,
        grad_t,
        halves,
        up_rows,
        pre_rows,
        load_sem,
        adj_sem,
        row_sem,
        list_send,
        list_recv,
        list_local,
        flag_send,
        flag_recv,
        halo_send,
        halo_recv,
        core_send,
        core_recv,
        sum_send,
        sum_recv,
    ) = refs

    blocks = features.shape[0]
    tiles = sources.shape[1]
    hslice = upstream.shape[1]
    nodes = upstream.shape[0]
    row_steps = nodes // ROWS
    count = lax.axis_size("node")
    n, f = lax.axis_index("node"), lax.axis_index("feat")
    z, y, x = n // (SIDE * SIDE), (n // SIDE) % SIDE, n % SIDE
    upper, lower = lax.rem(n + 1, count), lax.rem(n + count - 1, count)

    def z_peer(d):
        return lax.rem(z + d, SIDE) * (SIDE * SIDE) + y * SIDE + x

    def y_peer(d):
        return z * (SIDE * SIDE) + lax.rem(y + d, SIDE) * SIDE + x

    def x_peer(d):
        return z * (SIDE * SIDE) + y * SIDE + lax.rem(x + d, SIDE)

    def remote(src, dst, send, recv, target):
        return pltpu.make_async_remote_copy(
            src_ref=src, dst_ref=dst, send_sem=send, recv_sem=recv, device_id=target, device_id_type=MESH
        )

    columns = [features.at[:, :, pl.ds(k * COLS, COLS)] for k in range(stages)]
    own_load = [pltpu.make_async_copy(columns[k], own[k], load_sem.at[k, 0]) for k in range(stages)]
    pool_load = [
        pltpu.make_async_copy(columns[k], pool[k].at[pl.ds(cap, blocks)], load_sem.at[k, 1]) for k in range(stages)
    ]
    adj_load = pltpu.make_async_copy(adj_hbm, adj, adj_sem)

    def row_loads(step, slot):
        rows = pl.ds(pl.multiple_of(step * ROWS, ROWS), ROWS)
        return (
            pltpu.make_async_copy(upstream.at[rows], up_rows.at[slot], row_sem.at[slot, 0]),
            pltpu.make_async_copy(preact.at[rows], pre_rows.at[slot], row_sem.at[slot, 1]),
        )

    own_load[0].start()
    own_load[1].start()
    for copy in row_loads(0, 0):
        copy.start()
    barrier = pltpu.get_barrier_semaphore()
    greeted = [(upper, f), (lower, f), (n, 1 - f)]
    for d in range(1, SIDE):
        greeted += [(z_peer(d), f), (y_peer(d), f), (x_peer(d), f)]
    for target in greeted:
        pl.semaphore_signal(barrier, inc=1, device_id=target, device_id_type=MESH)

    found[...] = jnp.full(found.shape, -1, jnp.int32)
    found[0:1, 0:tiles] = sources[...]
    from_lower, from_upper, spots, excess = request(skip, cap, blocks, found[0:1, :])
    ask_lower[...] = jnp.broadcast_to(from_lower, ask_lower.shape)
    ask_upper[...] = jnp.broadcast_to(from_upper, ask_upper.shape)
    found[...] = jnp.broadcast_to(spots, found.shape)
    flag[0][...] = jnp.broadcast_to(excess, flag[0].shape)

    pl.semaphore_wait(barrier, len(greeted))
    ask = (
        remote(ask_lower, asked_by_upper, list_send.at[0], list_recv.at[0], (lower, f)),
        remote(ask_upper, asked_by_lower, list_send.at[1], list_recv.at[1], (upper, f)),
    )
    for copy in ask:
        copy.start()
    place_local = pltpu.make_async_copy(found, where, list_local.at[2])
    place_local.start()

    peers = (z_peer, y_peer, x_peer)
    position = (z, y, x)
    flags = [
        [
            remote(
                flag[phase],
                flag_in[phase].at[d - 1],
                flag_send.at[phase, d - 1],
                flag_recv.at[phase, d - 1],
                (peers[phase](d), f),
            )
            for d in range(1, SIDE)
        ]
        for phase in range(3)
    ]

    def flag_total(phase):
        for copy in flags[phase]:
            copy.wait_recv()
        return flag[phase][...] + flag_in[phase][0] + flag_in[phase][1] + flag_in[phase][2]

    ask[0].wait_recv()
    local_upper = pltpu.make_async_copy(asked_by_upper, to_upper, list_local.at[0])
    local_upper.start()
    ask[1].wait_recv()
    local_lower = pltpu.make_async_copy(asked_by_lower, to_lower, list_local.at[1])
    local_lower.start()
    local_upper.wait()
    local_lower.wait()

    halos = [
        (
            remote(up_buf[k], pool[k].at[pl.ds(0, cap)], halo_send.at[k, 0], halo_recv.at[k, 0], (upper, f)),
            remote(low_buf[k], pool[k].at[pl.ds(cap + blocks, cap)], halo_send.at[k, 1], halo_recv.at[k, 1], (lower, f)),
        )
        for k in range(stages)
    ]

    def pack(k):
        own_load[k].wait()

        def one(c, carry):
            up_buf[k][c] = own[k][within(to_upper[0, c], blocks)]
            low_buf[k][c] = own[k][within(to_lower[0, c], blocks)]
            return carry

        lax.fori_loop(0, cap, one, 0, unroll=2)

    for k in range(stages):
        pack(k)
        for copy in halos[k]:
            copy.start()
        if k == 0:
            for later in range(2, stages):
                own_load[later].start()
    adj_load.start()
    for k in range(stages):
        pool_load[k].start()
        pool[k][blocks + 2 * cap] = jnp.zeros((TILE, COLS), jnp.bfloat16)

    mine = pl.ds(pl.multiple_of(f * hslice, hslice), hslice)

    def core_copy(step):
        part = grad_t.at[mine, pl.ds(pl.multiple_of(step * ROWS, ROWS), ROWS)]
        return remote(part, part, core_send.at[step], core_recv.at[step], (n, 1 - f))

    def mask_step(step, carry):
        slot = lax.rem(step, 2)

        @pl.when(step + 1 < row_steps)
        def _():
            for copy in row_loads(step + 1, 1 - slot):
                copy.start()

        for copy in row_loads(step, slot):
            copy.wait()
        kept = jnp.where(pre_rows[slot].astype(jnp.float32) > 0.0, up_rows[slot].astype(jnp.float32), 0.0)
        grad_t[mine, pl.ds(pl.multiple_of(step * ROWS, ROWS), ROWS)] = kept.astype(jnp.bfloat16).T
        core_copy(step).start()
        return carry

    lax.fori_loop(0, row_steps, mask_step, 0)
    adj_load.wait()
    for k in range(stages):
        pool_load[k].wait()

    def core_wait(step, carry):
        core_copy(step).wait()
        return carry

    lax.fori_loop(0, row_steps, core_wait, 0)
    place_local.wait()

    sent = []

    def buffers(i):
        first_in, first_sum, second_in, second_sum, third_in = sums[5 * i : 5 * i + 5]
        return (first_in, second_in, third_in), (None, first_sum, second_sum)

    def source(i, phase, place):
        stage, low, rows, order = PARTS[i]
        if phase == 0:
            spot = [slice(None)] * 3
            spot[order[0]] = place
            return partial[stage], tuple(spot) + (pl.ds(low, rows),)
        held = buffers(i)[1][phase]
        if phase == 1 and order[1] == max(order[1:]):
            return held, (slice(None), place)
        return held, (place,)

    arriving = {}

    def send(i, phase):
        axis = PARTS[i][3][phase]
        arriving[i] = []
        for d in (2, 1, 3):
            ref, spot = source(i, phase, lax.rem(position[axis] + d, SIDE))
            copy = remote(
                ref.at[spot],
                buffers(i)[0][phase].at[d - 1],
                sum_send.at[i, phase, d - 1],
                sum_recv.at[i, phase, d - 1],
                (peers[axis](d), f),
            )
            copy.start()
            arriving[i].append(copy)
        sent.extend(arriving[i])

    def total(i, phase):
        for copy in arriving[i]:
            copy.wait_recv()
        ref, spot = source(i, phase, position[PARTS[i][3][phase]])
        got = buffers(i)[0][phase]
        return ref[spot] + got[0] + got[1] + got[2]

    z_shape = partial[0].shape[1:]
    z_rows = z_shape[0] * z_shape[1] * z_shape[2]

    def multiply(k):
        def one(place, carry):
            rows = pl.ds(pl.multiple_of(place * z_rows, z_rows), z_rows)
            both = jnp.dot(grad_t[rows, :], halves[...], preferred_element_type=jnp.float32)
            partial[k][place] = (both[:, :COLS] + both[:, COLS:]).reshape(z_shape)
            return carry

        lax.fori_loop(0, SIDE, one, 0)

    for k in range(stages):
        for copy in halos[k]:
            copy.wait_recv()
        if k == stages - 1:
            for i in range(len(PARTS)):
                if PARTS[i][0] != k:
                    send(i, 0)
            for copy in flags[0]:
                copy.start()

        def aggregate(b, carry):
            pair = jnp.concatenate([adj[2 * b], adj[2 * b + 1]], axis=1)
            left = within(where[0, 2 * b], blocks + 2 * cap + 1)
            right = within(where[0, 2 * b + 1], blocks + 2 * cap + 1)
            inputs = jnp.concatenate([pool[k][left], pool[k][right]], axis=0)
            total = jnp.dot(pair, inputs, preferred_element_type=jnp.float32)
            high = total.astype(jnp.bfloat16)
            low = (total - high.astype(jnp.float32)).astype(jnp.bfloat16)
            rows = pl.ds(pl.multiple_of(b * TILE, TILE), TILE)
            halves[rows, 0:COLS] = high
            halves[rows, COLS : 2 * COLS] = low
            return carry

        lax.fori_loop(0, blocks, aggregate, 0, unroll=8)
        multiply(k)
    for i in range(len(PARTS)):
        if PARTS[i][0] == stages - 1:
            send(i, 0)
    for phase in (1, 2):
        for i in range(len(PARTS)):
            buffers(i)[1][phase][...] = total(i, phase - 1)
            send(i, phase)
        flag[phase][...] = flag_total(phase - 1)
        for copy in flags[phase]:
            copy.start()
    for i in range(len(PARTS)):
        stage, low, rows, _ = PARTS[i]
        out[low : low + rows, stage * COLS : (stage + 1) * COLS] = total(i, 2)
    over[0, 0] = jnp.max(flag_total(2))
    for copy in sent:
        copy.wait_send()
    for pair in halos + [ask] + flags:
        for copy in pair:
            copy.wait_send()


def fused(skip, cap, collective_id, features, upstream, preact, adj_tiles, sources):
    nodes, fslice = features.shape
    hslice = upstream.shape[1]
    hidden = 2 * hslice
    blocks = nodes // TILE
    stages = fslice // COLS
    width = hidden // lax.axis_size("node")
    f32, bf16, i32 = jnp.float32, jnp.bfloat16, jnp.int32
    peers = SIDE - 1
    steps = nodes // ROWS

    def each(shape, dtype, times=stages):
        return [pltpu.VMEM(shape, dtype)] * times

    def sems(*shape):
        return pltpu.SemaphoreType.DMA(shape)

    sums = []
    for _, _, rows, _ in PARTS:
        sums += [
            pltpu.VMEM((peers, SIDE, SIDE, rows, COLS), f32),
            pltpu.VMEM((SIDE, SIDE, rows, COLS), f32),
            pltpu.VMEM((peers, SIDE, rows, COLS), f32),
            pltpu.VMEM((SIDE, rows, COLS), f32),
            pltpu.VMEM((peers, rows, COLS), f32),
        ]

    scratch = (
        each((blocks, TILE, COLS), bf16)
        + each((blocks + 2 * cap + 1, TILE, COLS), bf16)
        + each((cap, TILE, COLS), bf16)
        + each((cap, TILE, COLS), bf16)
        + each((SIDE, SIDE, SIDE, width, COLS), f32)
        + sums
        + each((peers, 8, LANES), f32, 3)
        + each((8, LANES), f32, 3)
        + each((8, LANES), i32, 5)
        + [pltpu.SMEM((8, LANES), i32)] * 3
        + [
            pltpu.VMEM(adj_tiles.shape, bf16),
            pltpu.VMEM((hidden, nodes), bf16),
            pltpu.VMEM((nodes, 2 * COLS), bf16),
            pltpu.VMEM((2, ROWS, hslice), bf16),
            pltpu.VMEM((2, ROWS, hslice), bf16),
            sems(stages, 2),
            pltpu.SemaphoreType.DMA,
            sems(2, 2),
            sems(2),
            sems(2),
            sems(3),
            sems(3, peers),
            sems(3, peers),
            sems(stages, 2),
            sems(stages, 2),
            sems(steps),
            sems(steps),
            sems(len(PARTS), 3, peers),
            sems(len(PARTS), 3, peers),
        ]
    )
    in_hbm = pl.BlockSpec(memory_space=pl.ANY)
    in_vmem = pl.BlockSpec(memory_space=pltpu.VMEM)
    flops = 4 * nodes * fslice * hidden + 4 * nodes * TILE * fslice
    return pl.pallas_call(
        functools.partial(fused_kernel, skip, cap),
        out_shape=(jax.ShapeDtypeStruct((width, fslice), f32), jax.ShapeDtypeStruct((1, 1), f32)),
        in_specs=[in_hbm] * 4 + [in_vmem],
        out_specs=(in_vmem, pl.BlockSpec(memory_space=pltpu.SMEM)),
        scratch_shapes=scratch,
        cost_estimate=pl.CostEstimate(flops=flops, bytes_accessed=8 * nodes * fslice, transcendentals=0),
        compiler_params=pltpu.CompilerParams(
            collective_id=collective_id, has_side_effects=True, vmem_limit_bytes=62 * 1024 * 1024
        ),
    )(features.reshape(blocks, TILE, fslice), upstream, preact, adj_tiles, sources)


def local(features, upstream, preact, adj_tiles, tile_source):
    nodes = features.shape[0]
    blocks = nodes // TILE
    factor = float(nodes * lax.axis_size("node")) ** (-0.5)
    args = (features, upstream, preact, adj_tiles, tile_source.reshape(1, -1))
    summed, over = fused(0, CAPACITY, 0, *args)
    summed = lax.cond(
        over[0, 0] > 0.0, lambda: summed + fused(CAPACITY, blocks - CAPACITY, 1, *args)[0], lambda: summed
    )
    return summed.T * factor


def solution(mesh):
    in_specs = (
        P("node", "feat"),
        P("node", "feat"),
        P("node", "feat"),
        P("node", None, None),
        P("node"),
    )
    out_specs = P("feat", "node")
    return jax.shard_map(local, mesh=mesh, in_specs=in_specs, out_specs=out_specs, check_vma=False)
```
